32 devices in a mesh: row: 8 (over z, x), vec: 4 (over y, core).
Axes of the slice: x: 2, y: 2, z: 4, core: 2. Of those that a mesh axis runs over, the one named last changes fastest.
Arguments:
- vectors: float32 [16384, 1024], P('row', 'vec'), may hold values from -8 to 8
- hamiltonian: float32 [128, 12, 128, 128], P('row'), may hold values from -0.15 to 0.15, as said below
- column_blocks: int32 [128, 12], P('row'), may hold values from 0 to 127, as said below
- live_counts: int32 [128], P('row'), may hold values from 3 to 12
- lower_bound: float32 [1], replicated, may hold values from -0.85 to -0.65
- upper_bound: float32 [1], replicated, may hold values from 1.05 to 1.3
Outputs:
- filtered: float32 [16384, 1024], P('row', 'vec')
The draws below stay inside these ranges and needn't reach their ends.
Inputs may be any that keep to these rules, and one draw needn't show every extreme that they name: column_blocks[i, 0] = i, and every entry lies within 16 block rows of its row i, cyclically modulo 128; the distances 16 and -16 both occur. `hamiltonian`: H is symmetric: for every used slot of block row i that names column block j there is a used slot of block row j that names i and holds the transpose of its block, and slot 0 of every block row holds a symmetric block.
All inputs are finite; a program needn't handle non-finite values.
Results may differ from the reference program's by a relative error of at most 0.0003.
Values sent between devices are 32-bit elements; how exact they have to be, the bound alone decides.
A program may use at most 128 MiB of HBM per device.

```python
import math
import jax
import jax.numpy as jnp
from jax import lax

B = 128
K = 12
NV = 1024
NS_ITERS = 3
BR_DEV = 16
NB = 128
ROWS = 16384


def build_pattern(key):
    pattern_key = jax.random.fold_in(key, 7001)
    key_dist, key_centre, key_live, key_match = jax.random.split(pattern_key, 4)
    layer_count = (K - 2) // 2
    distances = jax.random.randint(key_dist, (layer_count,), 1, BR_DEV + 1).astype(jnp.int32)
    centre = jax.random.randint(key_centre, (), 0, NB).astype(jnp.int32)
    row_ids = jnp.arange(NB, dtype=jnp.int32)
    half_rows = NB // 2
    distance_to = jnp.abs(row_ids - centre)
    distance_to = jnp.minimum(distance_to, NB - distance_to)
    nearness = (half_rows - distance_to) * 1000 // half_rows
    weight_level = nearness * nearness // 1000
    weight_level = weight_level * weight_level // 1000
    threshold = 50 + 950 * weight_level // 1000
    live_draws = jax.random.randint(key_live, (layer_count, NB), 0, 1000)
    shift_live = (live_draws < threshold[None, :]).astype(jnp.int32)
    shift_live = shift_live.at[0].set(1)
    partner = jnp.where(row_ids // BR_DEV % 2 == 0, row_ids + BR_DEV, row_ids - BR_DEV).astype(jnp.int32)
    lower_end = jnp.minimum(row_ids, partner)
    match_draws = jax.random.randint(key_match, (NB,), 0, 1000)
    match_live = (match_draws < threshold).astype(jnp.int32)
    layer_ids = jnp.arange(layer_count, dtype=jnp.int32)
    antipode = (centre + half_rows) % NB
    anti_minus = (antipode - distances) % NB
    shift_live = shift_live.at[layer_ids[1:], antipode].set(0)
    shift_live = shift_live.at[layer_ids[1:], anti_minus[1:]].set(0)
    match_live = match_live.at[lower_end[antipode]].set(0)
    centre_minus = (centre - distances) % NB
    shift_live = shift_live.at[layer_ids, centre].set(1)
    shift_live = shift_live.at[layer_ids, centre_minus].set(1)
    match_live = match_live.at[lower_end[centre]].set(1)
    plus_targets = (row_ids[:, None] + distances[None, :]) % NB
    minus_targets = (row_ids[:, None] - distances[None, :]) % NB
    targets = jnp.concatenate([row_ids[:, None], plus_targets, minus_targets, partner[:, None]], axis=1)
    plus_flags = shift_live.T
    minus_flags = shift_live[layer_ids[None, :], minus_targets]
    match_flags = match_live[lower_end][:, None]
    live_flags = jnp.concatenate([jnp.ones((NB, 1), jnp.int32), plus_flags, minus_flags, match_flags], axis=1)
    order_key = (1 - live_flags) * 16 + jnp.arange(K, dtype=jnp.int32)[None, :]
    slot_order = jnp.argsort(order_key, axis=1, stable=True).astype(jnp.int32)
    column_blocks = jnp.take_along_axis(targets, slot_order, axis=1).astype(jnp.int32)
    live_counts = jnp.sum(live_flags, axis=1).astype(jnp.int32)
    return (distances, partner, lower_end, minus_targets, slot_order, column_blocks, live_counts)


def draw_column_blocks(key, part):
    pattern = build_pattern(key)
    return pattern[5]


def draw_live_counts(key, part):
    pattern = build_pattern(key)
    return pattern[6]


def draw_hamiltonian(key, part):
    distances, partner, lower_end, minus_targets, slot_order, unused_cols, unused_counts = build_pattern(key)
    block_key = jax.random.fold_in(key, 7002)
    key_shift, key_match, key_self = jax.random.split(block_key, 3)
    layer_count = (K - 2) // 2
    block_scale = (4.0 * B * K) ** (-0.5)

    def entries(sub_key, array_shape):
        return jax.random.normal(sub_key, array_shape, jnp.float32)
    shift_blocks = entries(key_shift, (layer_count, NB, B, B))
    match_blocks = entries(key_match, (NB, B, B))
    self_raw = entries(key_self, (NB, B, B))
    row_ids = jnp.arange(NB, dtype=jnp.int32)
    layer_ids = jnp.arange(layer_count, dtype=jnp.int32)
    plus_blocks = jnp.moveaxis(shift_blocks, 0, 1)
    minus_blocks = jnp.swapaxes(shift_blocks[layer_ids[None, :], minus_targets], -1, -2)
    match_picked = match_blocks[lower_end]
    is_lower = (row_ids == lower_end)[:, None, None]
    match_side = jnp.where(is_lower, match_picked, jnp.swapaxes(match_picked, -1, -2))
    self_blocks = (self_raw + jnp.swapaxes(self_raw, -1, -2)) / math.sqrt(2.0)
    assembled = jnp.concatenate([self_blocks[:, None], plus_blocks, minus_blocks, match_side[:, None]], axis=1)
    assembled = jnp.clip(assembled * block_scale, -0.15, 0.15)
    return jnp.take_along_axis(assembled, slot_order[:, :, None, None], axis=1).astype(jnp.float32)


def draw_vectors(key, part):
    vector_key = jax.random.fold_in(key, 7003)
    key_base, key_mix = jax.random.split(vector_key, 2)
    base_rows = jax.random.normal(key_base, (ROWS, NV), jnp.float32)
    mixing = jax.random.normal(key_mix, (NV, NV), jnp.float32) * (0.5 / math.sqrt(NV))
    mixing = mixing + jnp.eye(NV, dtype=jnp.float32)
    mixed = jnp.dot(base_rows, mixing, precision=lax.Precision.HIGHEST)
    return jnp.clip(mixed, -8.0, 8.0).astype(jnp.float32)


def setup_inputs(seed: int = 0) -> dict:
    streams_of = jax.random.split(jax.random.key(seed), 7)
    vectors = draw_vectors(jax.random.fold_in(streams_of[6], 71), 0)
    hamiltonian = draw_hamiltonian(jax.random.fold_in(streams_of[6], 71), 0)
    column_blocks = draw_column_blocks(jax.random.fold_in(streams_of[6], 71), 0)
    live_counts = draw_live_counts(jax.random.fold_in(streams_of[6], 71), 0)
    lower_bound = jnp.clip(jax.random.uniform(streams_of[4], (1,), jnp.float32, -0.85, -0.65), -0.85, -0.65)
    upper_bound = jnp.clip(jax.random.uniform(streams_of[5], (1,), jnp.float32, 1.05, 1.3), 1.05, 1.3)
    return dict(vectors=vectors, hamiltonian=hamiltonian, column_blocks=column_blocks, live_counts=live_counts, lower_bound=lower_bound, upper_bound=upper_bound)


def apply_field(operand, hamiltonian, column_blocks, live_counts):
    blocks = operand.reshape(NB, B, NV)

    def add_slot(summed, inputs):
        matrix, targets, slot_index = inputs
        picked = jnp.take(blocks, targets, axis=0)
        live_mask = (slot_index < live_counts).astype(jnp.float32)
        summed = summed + jnp.einsum('rij,rjc->ric', matrix, picked * live_mask[:, None, None], precision=lax.Precision.HIGHEST)
        return (summed, None)
    inputs = (jnp.moveaxis(hamiltonian, 1, 0), column_blocks.T, jnp.arange(K, dtype=jnp.int32))
    summed, unused = lax.scan(add_slot, jnp.zeros((NB, B, NV), jnp.float32), inputs)
    return summed.reshape(ROWS, NV)

def reference(vectors, hamiltonian, column_blocks, live_counts, lower_bound, upper_bound):
    centre = (upper_bound[0] + lower_bound[0]) / 2
    radius = (upper_bound[0] - lower_bound[0]) / 2
    first = (apply_field(vectors, hamiltonian, column_blocks, live_counts) - centre * vectors) / radius
    second = 2 * (apply_field(first, hamiltonian, column_blocks, live_counts) - centre * first) / radius - vectors
    energy = jnp.sum(second * second)
    current = second * jnp.sqrt(NV / (4 * (energy + 1e-06)))
    for iteration in range(NS_ITERS):
        gram = jnp.einsum('rc,rd->cd', current, current, precision=lax.Precision.HIGHEST)
        current = 1.5 * current - 0.5 * jnp.dot(current, gram, precision=lax.Precision.HIGHEST, preferred_element_type=jnp.float32)
    return current * math.sqrt(ROWS)
```

```python
import functools
import math

import jax
import jax.numpy as jnp
from jax import lax
from jax.experimental import pallas as pl
from jax.experimental.pallas import tpu as pltpu
from jax.sharding import PartitionSpec as P

NS_ITERS = 3
PIECES = 4


def split(x):
    hi = x.astype(jnp.bfloat16)
    return hi, (x - hi.astype(jnp.float32)).astype(jnp.bfloat16)


def dot(a, b):
    return jnp.dot(a, b, preferred_element_type=jnp.float32)


def field_kernel(has_prev, pos_ref, live_ref, coef_ref, own_ref, near_ref, far_ref, ham_ref, *rest):
    if has_prev:
        prev_ref, out_ref, hi_ref, lo_ref = rest
    else:
        out_ref, hi_ref, lo_ref = rest
    i = pl.program_id(0)
    rows = own_ref.shape[0]
    slots, size = ham_ref.shape[1], ham_ref.shape[2]

    @pl.when(i == 0)
    def _():
        for part, ref in enumerate((own_ref, near_ref, far_ref)):
            @pl.loop(0, rows // size)
            def _(b):
                hi, lo = split(ref[pl.ds(pl.multiple_of(b * size, size), size), :])
                at = pl.multiple_of(part * rows + b * size, size)
                hi_ref[pl.ds(at, size), :] = hi
                lo_ref[pl.ds(at, size), :] = lo

    live = live_ref[i]
    acc_h = None
    for k in range(0, slots, 2):
        mats = [jnp.where(s < live, ham_ref[0, s], 0.0) for s in range(k, min(k + 2, slots))]
        spots = [pl.ds(pl.multiple_of(pos_ref[i, s] * size, size), size) for s in range(k, min(k + 2, slots))]
        mhi, mlo = split(jnp.concatenate(mats, axis=1))
        vhi = jnp.concatenate([hi_ref[s, :] for s in spots], axis=0)
        vlo = jnp.concatenate([lo_ref[s, :] for s in spots], axis=0)
        both = dot(jnp.concatenate([mhi, mlo], axis=0), vhi)
        term = both[:size] + both[size:] + dot(mhi, vlo)
        acc_h = term if acc_h is None else acc_h + term
    mine = pl.ds(pl.multiple_of(i * size, size), size)
    out = (acc_h - coef_ref[0] * own_ref[mine, :]) / coef_ref[1]
    if has_prev:
        out = 2 * out - prev_ref[...]
    out_ref[...] = out


def apply_field(pos, live, coef, own, near, far, ham, prev=None):
    rows, cols = own.shape
    block_rows, slots, size, _ = ham.shape
    whole = pl.BlockSpec(memory_space=pltpu.VMEM)
    smem = pl.BlockSpec(memory_space=pltpu.SMEM)
    one = pl.BlockSpec((size, cols), lambda i: (i, 0))
    specs = [smem, smem, smem, whole, whole, whole, pl.BlockSpec((1, slots, size, size), lambda i: (i, 0, 0, 0))]
    args = [pos, live, coef, own, near, far, ham]
    if prev is not None:
        specs.append(one)
        args.append(prev)
    return pl.pallas_call(
        functools.partial(field_kernel, prev is not None),
        grid=(block_rows,),
        out_shape=jax.ShapeDtypeStruct((rows, cols), jnp.float32),
        in_specs=specs,
        out_specs=one,
        scratch_shapes=[pltpu.VMEM((3 * rows, cols), jnp.bfloat16)] * 2,
        compiler_params=pltpu.CompilerParams(vmem_limit_bytes=40 * 1024 * 1024),
    )(*args)


def halo(x, count):
    rows = x.shape[0] // PIECES
    swap = [(r, r ^ 1) for r in range(count)]
    pass_on = [(r, (r + 2) % count if r % 2 == 0 else (r - 2) % count) for r in range(count)]
    near = [lax.ppermute(x[p * rows:(p + 1) * rows], "row", swap) for p in range(PIECES)]
    far = [lax.ppermute(p, "row", pass_on) for p in near]
    return jnp.concatenate(near), jnp.concatenate(far)


def on_device(vectors, hamiltonian, column_blocks, live_counts, lower_bound, upper_bound):
    rows_dev, panel_cols = vectors.shape
    block_rows = hamiltonian.shape[0]
    row_count = lax.axis_size("row")
    vec_count = lax.axis_size("vec")
    me = lax.axis_index("row")
    all_cols = panel_cols * vec_count

    rel = (column_blocks - me * block_rows + block_rows) % (block_rows * row_count)
    side = rel // block_rows
    part = jnp.where(side == 1, 0, jnp.where((side == 2) == (me % 2 == 0), 1, 2))
    pos = part * block_rows + rel % block_rows
    centre = (upper_bound[0] + lower_bound[0]) / 2
    radius = (upper_bound[0] - lower_bound[0]) / 2
    coef = jnp.stack([centre, radius])

    near, far = halo(vectors, row_count)
    first = apply_field(pos, live_counts, coef, vectors, near, far, hamiltonian)
    near, far = halo(first, row_count)
    second = apply_field(pos, live_counts, coef, first, near, far, hamiltonian, vectors)

    high = lax.Precision.HIGH
    full_rows = lax.all_gather(second, "vec", axis=1, tiled=True)
    panel = lax.dot_general(full_rows, second, (((0,), (0,)), ((), ())), precision=high, preferred_element_type=jnp.float32)
    panel = lax.psum(panel, "row")
    gram = lax.all_gather(panel, "vec", axis=1, tiled=True)
    energy = jnp.trace(gram)
    scale2 = all_cols / (4 * (energy + 1e-06))
    gram = gram * scale2
    column = jnp.arange(panel_cols)[None, :] + lax.axis_index("vec") * panel_cols
    eye = (jnp.arange(all_cols)[:, None] == column).astype(jnp.float32)

    def times_gram(level, x):
        if level == 0:
            return jnp.dot(gram, x, precision=high)
        return times_gram(level - 1, times_step(level - 1, times_step(level - 1, x)))

    def times_step(level, x):
        return 1.5 * x - 0.5 * times_gram(level, x)

    poly = 1.5 * eye - 0.5 * panel * scale2
    for level in range(1, NS_ITERS):
        poly = times_step(level, poly)
    poly = poly * (jnp.sqrt(scale2) * math.sqrt(rows_dev * row_count))
    return jnp.dot(full_rows, poly, precision=high)


def solution(mesh):
    placed = (P("row", "vec"), P("row", None, None, None), P("row", None), P("row"), P(), P())
    return jax.shard_map(
        on_device, mesh=mesh, in_specs=placed, out_specs=P("row", "vec"), check_vma=False
    )
```

```python
import functools
import math

import jax
import jax.numpy as jnp
from jax import lax
from jax.experimental import pallas as pl
from jax.experimental.pallas import tpu as pltpu
from jax.sharding import PartitionSpec as P

NS_ITERS = 3
PIECES = 4
MESH = pl.DeviceIdType.MESH


def split(x):
    hi = x.astype(jnp.bfloat16)
    return hi, (x - hi.astype(jnp.float32)).astype(jnp.bfloat16)


def dot(a, b):
    return jnp.dot(a, b, preferred_element_type=jnp.float32)


def filter_kernel(row_count, vec_count, width, pos_ref, live_ref, coef_ref, vec_ref, ham_ref, full_ref,
                  ham, mats, near, far, first, hi_ref, lo_ref, ham_sem,
                  swap_send, swap_recv, pass_send, pass_recv, side_send, side_recv, over_send, over_recv,
                  relay_send, relay_recv):
    row, vec = lax.axis_index("row"), lax.axis_index("vec")
    rows, cols = vec_ref.shape
    block_rows, slots, size, _ = ham.shape
    chunks = cols // width
    piece = rows // PIECES
    even = 1 - row % 2
    partner = row + 2 * even - 1
    onward = (row + 4 * even - 2 + row_count) % row_count
    backward = (row - 4 * even + 2 + row_count) % row_count
    sibling = vec + 1 - 2 * (vec % 2)
    overs = [(vec + 2 * d) % vec_count for d in range(1, vec_count // 2)]
    sources = [(vec - 2 * d + vec_count) % vec_count for d in range(1, vec_count // 2)]

    copy = pltpu.make_async_copy(ham_ref, ham, ham_sem)
    copy.start()
    barrier = pltpu.get_barrier_semaphore()
    peers = [(partner, vec), (onward, vec), (backward, vec), (row, sibling)] + [(row, v) for v in overs]
    for peer in peers:
        pl.semaphore_signal(barrier, inc=1, device_id=peer, device_id_type=MESH)
    pl.semaphore_wait(barrier, len(peers))

    def part(q):
        return pl.ds(q * piece, piece)

    def columns(c, v):
        return pl.ds(pl.multiple_of((c * vec_count + v) * width, width), width)

    def own_at(stage, c, q):
        return first.at[c, part(q)] if stage else vec_ref.at[part(q), pl.ds(c * width, width)]

    def swap(stage, c, q):
        return pltpu.make_async_remote_copy(
            own_at(stage, c, q), near.at[stage, c, part(q)], swap_send.at[stage, c, q], swap_recv.at[stage, c, q],
            device_id=(partner, vec), device_id_type=MESH)

    def pass_on(stage, c, q):
        return pltpu.make_async_remote_copy(
            near.at[stage, c, part(q)], far.at[stage, c, part(q)], pass_send.at[stage, c, q],
            pass_recv.at[stage, c, q], device_id=(onward, vec), device_id_type=MESH)

    def across(c, q, v, send, recv, to):
        at = full_ref.at[part(q), columns(c, v)]
        return pltpu.make_async_remote_copy(at, at, send, recv, device_id=(row, to), device_id_type=MESH)

    def side(c, q):
        return across(c, q, vec, side_send.at[c, q], side_recv.at[c, q], sibling)

    def over(c, q, d):
        return across(c, q, vec, over_send.at[c, q, d], over_recv.at[c, q, d], overs[d])

    def relay(c, q, d):
        return across(c, q, sources[d], relay_send.at[c, q, d], relay_recv.at[c, q, d], sibling)

    every = [(c, q) for c in range(chunks) for q in range(PIECES)]
    for c, q in every:
        swap(0, c, q).start()

    copy.wait()

    @pl.loop(0, block_rows)
    def _(i):
        for k in range(0, slots, 2):
            pair = [ham[i, s] * live_ref[i, s] for s in (k, k + 1)]
            hi, lo = split(jnp.concatenate(pair, axis=1))
            mats[i, k // 2, pl.ds(0, size), :] = hi
            mats[i, k // 2, pl.ds(size, size), :] = lo

    def spread(read, place, q):
        @pl.loop(0, piece // size)
        def _(b):
            at = pl.multiple_of(q * piece + b * size, size)
            hi, lo = split(read(pl.ds(at, size)))
            to = (place * rows + q * piece) // size + b
            hi_ref[to] = hi
            lo_ref[to] = lo

    for stage in range(2):
        for c in range(chunks):
            wide = pl.ds(c * width, width)

            def own(at):
                return first[c, at, :] if stage else vec_ref[at, wide]

            for q in range(PIECES):
                spread(own, 0, q)
            for q in range(PIECES):
                swap(stage, c, q).wait_recv()
                pass_on(stage, c, q).start()
                spread(lambda at: near[stage, c, at, :], 1, q)
            for q in range(PIECES):
                pass_on(stage, c, q).wait_recv()
                spread(lambda at: far[stage, c, at, :], 2, q)

            @pl.loop(0, block_rows)
            def _(i):
                total = jnp.zeros((size, width), jnp.float32)
                for k in range(0, slots, 2):
                    vhi = jnp.concatenate([hi_ref[pos_ref[i, s]] for s in (k, k + 1)], axis=0)
                    vlo = jnp.concatenate([lo_ref[pos_ref[i, s]] for s in (k, k + 1)], axis=0)
                    both = dot(mats[i, k // 2], vhi)
                    total += both[:size] + both[size:] + dot(mats[i, k // 2, pl.ds(0, size), :], vlo)
                at = pl.ds(pl.multiple_of(i * size, size), size)
                out = (total - coef_ref[0] * own(at)) / coef_ref[1]
                if stage:
                    full_ref[at, columns(c, vec)] = 2 * out - vec_ref[at, wide]
                else:
                    first[c, at, :] = out

            for q in range(PIECES):
                if stage:
                    for d in range(len(overs)):
                        over(c, q, d).start()
                    side(c, q).start()
                else:
                    swap(1, c, q).start()

    for c, q in every:
        for d in range(len(overs)):
            over(c, q, d).wait_recv()
            relay(c, q, d).start()
    for c, q in every:
        side(c, q).wait()
        for d in range(len(overs)):
            over(c, q, d).wait_send()
            relay(c, q, d).wait()
        for stage in range(2):
            swap(stage, c, q).wait_send()
            pass_on(stage, c, q).wait_send()


def filtered_rows(row_count, vec_count, width, pos, live, coef, vectors, ham):
    rows, cols = vectors.shape
    block_rows, slots, size, _ = ham.shape
    chunks = cols // width
    smem = pl.BlockSpec(memory_space=pltpu.SMEM)
    vmem = pl.BlockSpec(memory_space=pltpu.VMEM)
    dma = pltpu.SemaphoreType.DMA
    others = max(1, vec_count // 2 - 1)
    return pl.pallas_call(
        functools.partial(filter_kernel, row_count, vec_count, width),
        out_shape=jax.ShapeDtypeStruct((rows, cols * vec_count), jnp.float32),
        in_specs=[smem, smem, smem, vmem, pl.BlockSpec(memory_space=pl.ANY)],
        out_specs=vmem,
        scratch_shapes=[
            pltpu.VMEM(ham.shape, jnp.float32),
            pltpu.VMEM((block_rows, slots // 2, 2 * size, 2 * size), jnp.bfloat16),
            pltpu.VMEM((2, chunks, rows, width), jnp.float32),
            pltpu.VMEM((2, chunks, rows, width), jnp.float32),
            pltpu.VMEM((chunks, rows, width), jnp.float32),
            pltpu.VMEM((3 * block_rows, size, width), jnp.bfloat16),
            pltpu.VMEM((3 * block_rows, size, width), jnp.bfloat16),
            dma,
            dma((2, chunks, PIECES)), dma((2, chunks, PIECES)),
            dma((2, chunks, PIECES)), dma((2, chunks, PIECES)),
            dma((chunks, PIECES)), dma((chunks, PIECES)),
            dma((chunks, PIECES, others)), dma((chunks, PIECES, others)),
            dma((chunks, PIECES, others)), dma((chunks, PIECES, others)),
        ],
        compiler_params=pltpu.CompilerParams(
            collective_id=0, has_side_effects=True, vmem_limit_bytes=58 * 1024 * 1024
        ),
    )(pos, live, coef, vectors, ham)


def on_device(vectors, hamiltonian, column_blocks, live_counts, lower_bound, upper_bound):
    rows_dev, panel_cols = vectors.shape
    block_rows = hamiltonian.shape[0]
    row_count = lax.axis_size("row")
    vec_count = lax.axis_size("vec")
    me = lax.axis_index("row")
    all_cols = panel_cols * vec_count

    rel = (column_blocks - me * block_rows + block_rows) % (block_rows * row_count)
    side = rel // block_rows
    part = jnp.where(side == 1, 0, jnp.where((side == 2) == (me % 2 == 0), 1, 2))
    pos = part * block_rows + rel % block_rows
    slots = column_blocks.shape[1]
    live = (jnp.arange(slots, dtype=jnp.int32)[None, :] < live_counts[:, None]).astype(jnp.float32)
    centre = (upper_bound[0] + lower_bound[0]) / 2
    radius = (upper_bound[0] - lower_bound[0]) / 2
    coef = jnp.stack([centre, radius])

    width = max(128, panel_cols // 2)
    full_rows = filtered_rows(
        row_count, vec_count, width, pos, live, coef, vectors, hamiltonian
    )

    high = lax.Precision.HIGH
    span = width * vec_count
    own = jnp.concatenate([
        lax.dynamic_slice_in_dim(full_rows, c * span + lax.axis_index("vec") * width, width, axis=1)
        for c in range(panel_cols // width)
    ], axis=1)
    panel = lax.dot_general(
        full_rows, own, (((0,), (0,)), ((), ())), precision=high, preferred_element_type=jnp.float32
    )
    panel = lax.psum(panel, "row")
    panels = lax.all_gather(panel, "vec")
    gram = jnp.concatenate(
        [panels[v][:, c:c + width] for c in range(0, panel_cols, width) for v in range(vec_count)], axis=1
    )
    energy = jnp.trace(gram)
    scale2 = all_cols / (4 * (energy + 1e-06))
    gram = gram * scale2
    local = jnp.arange(panel_cols)
    column = local // width * (width * vec_count) + lax.axis_index("vec") * width + local % width
    eye = (jnp.arange(all_cols)[:, None] == column[None, :]).astype(jnp.float32)

    def times_gram(level, x):
        if level == 0:
            return jnp.dot(gram, x, precision=high)
        return times_gram(level - 1, times_step(level - 1, times_step(level - 1, x)))

    def times_step(level, x):
        return 1.5 * x - 0.5 * times_gram(level, x)

    poly = 1.5 * eye - 0.5 * panel * scale2
    for level in range(1, NS_ITERS):
        poly = times_step(level, poly)
    poly = poly * (jnp.sqrt(scale2) * math.sqrt(rows_dev * row_count))
    return jnp.dot(full_rows, poly, precision=high)


def solution(mesh):
    placed = (P("row", "vec"), P("row", None, None, None), P("row", None), P("row"), P(), P())
    return jax.shard_map(
        on_device, mesh=mesh, in_specs=placed, out_specs=P("row", "vec"), check_vma=False
    )
```

```python
import functools
import math

import jax
import jax.numpy as jnp
from jax import lax
from jax.experimental import pallas as pl
from jax.experimental.pallas import tpu as pltpu
from jax.sharding import PartitionSpec as P

NS_ITERS = 3
PIECES = 4
MESH = pl.DeviceIdType.MESH


def split(x):
    hi = x.astype(jnp.bfloat16)
    return hi, (x - hi.astype(jnp.float32)).astype(jnp.bfloat16)


def dot(a, b):
    return jnp.dot(a, b, preferred_element_type=jnp.float32)


def filter_kernel(row_count, vec_count, width, pos_ref, live_ref, coef_ref, vec_ref, ham_ref, full_ref,
                  ham, mats, near, far, first, hi_ref, lo_ref, ham_sem,
                  swap_send, swap_recv, pass_send, pass_recv, side_send, side_recv, over_send, over_recv,
                  relay_send, relay_recv):
    row, vec = lax.axis_index("row"), lax.axis_index("vec")
    rows, cols = vec_ref.shape
    block_rows, slots, size, _ = ham.shape
    chunks = cols // width
    piece = rows // PIECES
    even = 1 - row % 2
    partner = row + 2 * even - 1
    onward = (row + 4 * even - 2 + row_count) % row_count
    backward = (row - 4 * even + 2 + row_count) % row_count
    sibling = vec + 1 - 2 * (vec % 2)
    overs = [(vec + 2 * d) % vec_count for d in range(1, vec_count // 2)]
    sources = [(vec - 2 * d + vec_count) % vec_count for d in range(1, vec_count // 2)]

    copy = pltpu.make_async_copy(ham_ref, ham, ham_sem)
    copy.start()
    barrier = pltpu.get_barrier_semaphore()
    peers = [(partner, vec), (onward, vec), (backward, vec), (row, sibling)] + [(row, v) for v in overs]
    for peer in peers:
        pl.semaphore_signal(barrier, inc=1, device_id=peer, device_id_type=MESH)
    pl.semaphore_wait(barrier, len(peers))

    def part(q):
        return pl.ds(q * piece, piece)

    def columns(c, v):
        return pl.ds(pl.multiple_of((c * vec_count + v) * width, width), width)

    def own_at(stage, c, q):
        return first.at[c, part(q)] if stage else vec_ref.at[part(q), pl.ds(c * width, width)]

    def swap(stage, c, q):
        return pltpu.make_async_remote_copy(
            own_at(stage, c, q), near.at[stage, c, part(q)], swap_send.at[stage, c, q], swap_recv.at[stage, c, q],
            device_id=(partner, vec), device_id_type=MESH)

    def pass_on(stage, c, q):
        return pltpu.make_async_remote_copy(
            near.at[stage, c, part(q)], far.at[stage, c, part(q)], pass_send.at[stage, c, q],
            pass_recv.at[stage, c, q], device_id=(onward, vec), device_id_type=MESH)

    def across(c, q, v, send, recv, to):
        at = full_ref.at[part(q), columns(c, v)]
        return pltpu.make_async_remote_copy(at, at, send, recv, device_id=(row, to), device_id_type=MESH)

    def side(c, q):
        return across(c, q, vec, side_send.at[c, q], side_recv.at[c, q], sibling)

    def over(c, q, d):
        return across(c, q, vec, over_send.at[c, q, d], over_recv.at[c, q, d], overs[d])

    def relay(c, q, d):
        return across(c, q, sources[d], relay_send.at[c, q, d], relay_recv.at[c, q, d], sibling)

    every = [(c, q) for c in range(chunks) for q in range(PIECES)]
    for c, q in every:
        swap(0, c, q).start()

    copy.wait()

    @pl.loop(0, block_rows)
    def _(i):
        for k in range(0, slots, 2):
            pair = [ham[i, s] * live_ref[i, s] for s in (k, k + 1)]
            hi, lo = split(jnp.concatenate(pair, axis=1))
            mats[i, k // 2, pl.ds(0, size), :] = hi
            mats[i, k // 2, pl.ds(size, size), :] = lo

    def spread(read, place, q):
        @pl.loop(0, piece // size)
        def _(b):
            at = pl.multiple_of(q * piece + b * size, size)
            hi, lo = split(read(pl.ds(at, size)))
            to = (place * rows + q * piece) // size + b
            hi_ref[to] = hi
            lo_ref[to] = lo

    for stage in range(2):
        for c in range(chunks):
            wide = pl.ds(c * width, width)

            def own(at):
                return first[c, at, :] if stage else vec_ref[at, wide]

            for q in range(PIECES):
                spread(own, 0, q)
            for q in range(PIECES):
                swap(stage, c, q).wait_recv()
                pass_on(stage, c, q).start()
                spread(lambda at: near[stage, c, at, :], 1, q)
            for q in range(PIECES):
                pass_on(stage, c, q).wait_recv()
                spread(lambda at: far[stage, c, at, :], 2, q)

            @pl.loop(0, block_rows)
            def _(i):
                total = jnp.zeros((size, width), jnp.float32)
                for k in range(0, slots, 2):
                    vhi = jnp.concatenate([hi_ref[pos_ref[i, s]] for s in (k, k + 1)], axis=0)
                    vlo = jnp.concatenate([lo_ref[pos_ref[i, s]] for s in (k, k + 1)], axis=0)
                    both = dot(mats[i, k // 2], vhi)
                    total += both[:size] + both[size:] + dot(mats[i, k // 2, pl.ds(0, size), :], vlo)
                at = pl.ds(pl.multiple_of(i * size, size), size)
                out = (total - coef_ref[0] * own(at)) / coef_ref[1]
                if stage:
                    full_ref[at, columns(c, vec)] = 2 * out - vec_ref[at, wide]
                else:
                    first[c, at, :] = out

            for q in range(PIECES):
                if stage:
                    for d in range(len(overs)):
                        over(c, q, d).start()
                    side(c, q).start()
                else:
                    swap(1, c, q).start()

    for c, q in every:
        for d in range(len(overs)):
            over(c, q, d).wait_recv()
            relay(c, q, d).start()
    for c, q in every:
        side(c, q).wait()
        for d in range(len(overs)):
            over(c, q, d).wait_send()
            relay(c, q, d).wait()
        for stage in range(2):
            swap(stage, c, q).wait_send()
            pass_on(stage, c, q).wait_send()


def filtered_rows(row_count, vec_count, width, pos, live, coef, vectors, ham):
    rows, cols = vectors.shape
    block_rows, slots, size, _ = ham.shape
    chunks = cols // width
    smem = pl.BlockSpec(memory_space=pltpu.SMEM)
    vmem = pl.BlockSpec(memory_space=pltpu.VMEM)
    dma = pltpu.SemaphoreType.DMA
    others = max(1, vec_count // 2 - 1)
    return pl.pallas_call(
        functools.partial(filter_kernel, row_count, vec_count, width),
        out_shape=jax.ShapeDtypeStruct((rows, cols * vec_count), jnp.float32),
        in_specs=[smem, smem, smem, vmem, pl.BlockSpec(memory_space=pl.ANY)],
        out_specs=vmem,
        scratch_shapes=[
            pltpu.VMEM(ham.shape, jnp.float32),
            pltpu.VMEM((block_rows, slots // 2, 2 * size, 2 * size), jnp.bfloat16),
            pltpu.VMEM((2, chunks, rows, width), jnp.float32),
            pltpu.VMEM((2, chunks, rows, width), jnp.float32),
            pltpu.VMEM((chunks, rows, width), jnp.float32),
            pltpu.VMEM((3 * block_rows, size, width), jnp.bfloat16),
            pltpu.VMEM((3 * block_rows, size, width), jnp.bfloat16),
            dma,
            dma((2, chunks, PIECES)), dma((2, chunks, PIECES)),
            dma((2, chunks, PIECES)), dma((2, chunks, PIECES)),
            dma((chunks, PIECES)), dma((chunks, PIECES)),
            dma((chunks, PIECES, others)), dma((chunks, PIECES, others)),
            dma((chunks, PIECES, others)), dma((chunks, PIECES, others)),
        ],
        compiler_params=pltpu.CompilerParams(
            collective_id=0, has_side_effects=True, vmem_limit_bytes=58 * 1024 * 1024
        ),
    )(pos, live, coef, vectors, ham)


def gram_kernel(row_count, vec_count, width, full_ref, gram_ref, hi_ref, lo_ref, own_ref, panel, inbox,
                sum_send, sum_recv, deep_send, deep_recv, swap_send, swap_recv, over_send, over_recv,
                side_send, side_recv):
    row, vec = lax.axis_index("row"), lax.axis_index("vec")
    rows, all_cols = full_ref.shape
    chunks, span = all_cols // vec_count // width, width * vec_count
    piece = panel.shape[0] // row_count
    pairs, groups = row_count // 2, vec_count // 2
    partner = row + 1 - 2 * (row % 2)
    sibling = vec + 1 - 2 * (vec % 2)

    barrier = pltpu.get_barrier_semaphore()
    peers = [((row + d) % row_count, vec) for d in range(1, row_count)]
    peers += [(row, (vec + 2 * d) % vec_count) for d in range(1, groups)] + [(row, sibling)]
    for peer in peers:
        pl.semaphore_signal(barrier, inc=1, device_id=peer, device_id_type=MESH)

    step = 128

    @pl.loop(0, rows // step)
    def _(b):
        at = pl.ds(pl.multiple_of(b * step, step), step)
        hi, lo = split(full_ref[at, :])
        hi_ref[at, :] = hi
        lo_ref[at, :] = lo
        for c in range(chunks):
            mine = full_ref[at, pl.ds(pl.multiple_of(c * span + vec * width, width), width)].T
            hi, lo = split(mine)
            own_ref[c, pl.ds(0, width), at] = hi
            own_ref[c, pl.ds(width, width), at] = lo

    def give(d):
        target = (row + d) % row_count
        return pltpu.make_async_remote_copy(
            panel.at[pl.ds(pl.multiple_of(target * piece, piece), piece)], inbox.at[d - 1],
            sum_send.at[d - 1], sum_recv.at[d - 1], device_id=(target, vec), device_id_type=MESH)

    tile = min(256, all_cols)
    for c in range(chunks):
        @pl.loop(0, all_cols // tile)
        def _(t):
            at = pl.ds(pl.multiple_of(t * tile, tile), tile)
            both = dot(own_ref[c], hi_ref[:, at])
            panel[pl.ds(c * width, width), at] = (
                both[:width] + both[width:] + dot(own_ref[c, pl.ds(0, width), :], lo_ref[:, at])
            )
    pl.semaphore_wait(barrier, len(peers))
    for d in range(1, row_count):
        give(d).start()

    def rows_of(r, v):
        local = r * piece
        return pl.ds(pl.multiple_of(local // width * span + v * width + local % width, piece), piece)

    def send(r, v, sems, index, to):
        at = gram_ref.at[rows_of(r, v)]
        return pltpu.make_async_remote_copy(
            at, at, sems[0].at[index], sems[1].at[index], device_id=to, device_id_type=MESH)

    def row_of(k, base):
        return (base + 2 * k) % row_count

    def deep(d):
        return send(row, vec, (deep_send, deep_recv), d - 1, (row_of(d, row), vec))

    def swap(k):
        return send(row_of(k, row), vec, (swap_send, swap_recv), k, (partner, vec))

    def held(k):
        return row_of(k, row) if k < pairs else row_of(k - pairs, partner)

    def over(k, d):
        return send(held(k), vec, (over_send, over_recv), (k, d - 1), (row, (vec + 2 * d) % vec_count))

    def side(k, d):
        return send(held(k), (vec + 2 * d) % vec_count, (side_send, side_recv), (k, d), (row, sibling))

    acc = panel[pl.ds(pl.multiple_of(row * piece, piece), piece), :]
    for d in range(1, row_count):
        give(d).wait_recv()
        acc = acc + inbox[d - 1]
    gram_ref[rows_of(row, vec), :] = acc
    for d in range(1, pairs):
        deep(d).start()

    def spread(k):
        for d in range(1, groups):
            over(k, d).start()
        side(k, 0).start()

    swap(0).start()
    spread(0)
    for d in range(1, pairs):
        deep(pairs - d).wait_recv()
        swap(d).start()
        spread(d)
    for k in range(pairs):
        swap(k).wait_recv()
        spread(pairs + k)
    for k in range(row_count):
        for d in range(1, groups):
            over(k, groups - d).wait_recv()
            side(k, d).start()
    for d in range(1, row_count):
        give(d).wait_send()
    for d in range(1, pairs):
        deep(d).wait_send()
    for k in range(pairs):
        swap(k).wait_send()
    for k in range(row_count):
        for d in range(1, groups):
            over(k, d).wait_send()
        for d in range(groups):
            side(k, d).wait()


def full_gram(row_count, vec_count, width, full):
    rows, all_cols = full.shape
    cols = all_cols // vec_count
    vmem = pl.BlockSpec(memory_space=pltpu.VMEM)
    dma = pltpu.SemaphoreType.DMA
    pairs, groups = row_count // 2, vec_count // 2
    others = max(1, groups - 1)
    return pl.pallas_call(
        functools.partial(gram_kernel, row_count, vec_count, width),
        out_shape=jax.ShapeDtypeStruct((all_cols, all_cols), jnp.float32),
        in_specs=[vmem],
        out_specs=vmem,
        scratch_shapes=[
            pltpu.VMEM((rows, all_cols), jnp.bfloat16),
            pltpu.VMEM((rows, all_cols), jnp.bfloat16),
            pltpu.VMEM((cols // width, 2 * width, rows), jnp.bfloat16),
            pltpu.VMEM((cols, all_cols), jnp.float32),
            pltpu.VMEM((row_count - 1, cols // row_count, all_cols), jnp.float32),
            dma((row_count - 1,)), dma((row_count - 1,)),
            dma((max(1, pairs - 1),)), dma((max(1, pairs - 1),)),
            dma((pairs,)), dma((pairs,)),
            dma((row_count, others)), dma((row_count, others)),
            dma((row_count, groups)), dma((row_count, groups)),
        ],
        compiler_params=pltpu.CompilerParams(
            collective_id=1, has_side_effects=True, vmem_limit_bytes=50 * 1024 * 1024
        ),
    )(full)


def on_device(vectors, hamiltonian, column_blocks, live_counts, lower_bound, upper_bound):
    rows_dev, panel_cols = vectors.shape
    block_rows = hamiltonian.shape[0]
    row_count = lax.axis_size("row")
    vec_count = lax.axis_size("vec")
    me = lax.axis_index("row")
    all_cols = panel_cols * vec_count

    rel = (column_blocks - me * block_rows + block_rows) % (block_rows * row_count)
    side = rel // block_rows
    part = jnp.where(side == 1, 0, jnp.where((side == 2) == (me % 2 == 0), 1, 2))
    pos = part * block_rows + rel % block_rows
    slots = column_blocks.shape[1]
    live = (jnp.arange(slots, dtype=jnp.int32)[None, :] < live_counts[:, None]).astype(jnp.float32)
    centre = (upper_bound[0] + lower_bound[0]) / 2
    radius = (upper_bound[0] - lower_bound[0]) / 2
    coef = jnp.stack([centre, radius])

    width = max(128, panel_cols // 2)
    full_rows = filtered_rows(
        row_count, vec_count, width, pos, live, coef, vectors, hamiltonian
    )

    high = lax.Precision.HIGH
    span = width * vec_count
    gram = full_gram(row_count, vec_count, width, full_rows)
    panel = jnp.concatenate([
        lax.dynamic_slice_in_dim(gram, c * span + lax.axis_index("vec") * width, width, axis=1)
        for c in range(panel_cols // width)
    ], axis=1)
    energy = jnp.trace(gram)
    scale2 = all_cols / (4 * (energy + 1e-06))
    gram = gram * scale2
    local = jnp.arange(panel_cols)
    column = local // width * (width * vec_count) + lax.axis_index("vec") * width + local % width
    eye = (jnp.arange(all_cols)[:, None] == column[None, :]).astype(jnp.float32)

    def times_gram(level, x):
        if level == 0:
            return jnp.dot(gram, x, precision=high)
        return times_gram(level - 1, times_step(level - 1, times_step(level - 1, x)))

    def times_step(level, x):
        return 1.5 * x - 0.5 * times_gram(level, x)

    poly = 1.5 * eye - 0.5 * panel * scale2
    for level in range(1, NS_ITERS):
        poly = times_step(level, poly)
    poly = poly * (jnp.sqrt(scale2) * math.sqrt(rows_dev * row_count))
    return jnp.dot(full_rows, poly, precision=high)


def solution(mesh):
    placed = (P("row", "vec"), P("row", None, None, None), P("row", None), P("row"), P(), P())
    return jax.shard_map(
        on_device, mesh=mesh, in_specs=placed, out_specs=P("row", "vec"), check_vma=False
    )
```

```python
import functools
import math

import jax
import jax.numpy as jnp
from jax import lax
from jax.experimental import pallas as pl
from jax.experimental.pallas import tpu as pltpu
from jax.sharding import PartitionSpec as P

NS_ITERS = 3
PIECES = 4
MESH = pl.DeviceIdType.MESH


def split(x):
    hi = x.astype(jnp.bfloat16)
    return hi, (x - hi.astype(jnp.float32)).astype(jnp.bfloat16)


def dot(a, b):
    return jnp.dot(a, b, preferred_element_type=jnp.float32)


def filter_kernel(row_count, vec_count, width, pos_ref, live_ref, coef_ref, vec_ref, ham_ref, full_ref,
                  ham, mats, near, far, first, hi_ref, lo_ref, ham_sem,
                  swap_send, swap_recv, pass_send, pass_recv, side_send, side_recv, over_send, over_recv,
                  relay_send, relay_recv):
    row, vec = lax.axis_index("row"), lax.axis_index("vec")
    rows, cols = vec_ref.shape
    block_rows, slots, size, _ = ham.shape
    chunks = cols // width
    piece = rows // PIECES
    even = 1 - row % 2
    partner = row + 2 * even - 1
    onward = (row + 4 * even - 2 + row_count) % row_count
    backward = (row - 4 * even + 2 + row_count) % row_count
    sibling = vec + 1 - 2 * (vec % 2)
    overs = [(vec + 2 * d) % vec_count for d in range(1, vec_count // 2)]
    sources = [(vec - 2 * d + vec_count) % vec_count for d in range(1, vec_count // 2)]

    copy = pltpu.make_async_copy(ham_ref, ham, ham_sem)
    copy.start()
    barrier = pltpu.get_barrier_semaphore()
    peers = [(partner, vec), (onward, vec), (backward, vec), (row, sibling)] + [(row, v) for v in overs]
    for peer in peers:
        pl.semaphore_signal(barrier, inc=1, device_id=peer, device_id_type=MESH)
    pl.semaphore_wait(barrier, len(peers))

    def part(q):
        return pl.ds(q * piece, piece)

    def columns(c, v):
        return pl.ds(pl.multiple_of((c * vec_count + v) * width, width), width)

    def own_at(stage, c, q):
        return first.at[c, part(q)] if stage else vec_ref.at[part(q), pl.ds(c * width, width)]

    def swap(stage, c, q):
        return pltpu.make_async_remote_copy(
            own_at(stage, c, q), near.at[stage, c, part(q)], swap_send.at[stage, c, q], swap_recv.at[stage, c, q],
            device_id=(partner, vec), device_id_type=MESH)

    def pass_on(stage, c, q):
        return pltpu.make_async_remote_copy(
            near.at[stage, c, part(q)], far.at[stage, c, part(q)], pass_send.at[stage, c, q],
            pass_recv.at[stage, c, q], device_id=(onward, vec), device_id_type=MESH)

    def across(c, q, v, send, recv, to):
        at = full_ref.at[part(q), columns(c, v)]
        return pltpu.make_async_remote_copy(at, at, send, recv, device_id=(row, to), device_id_type=MESH)

    def side(c, q):
        return across(c, q, vec, side_send.at[c, q], side_recv.at[c, q], sibling)

    def over(c, q, d):
        return across(c, q, vec, over_send.at[c, q, d], over_recv.at[c, q, d], overs[d])

    def relay(c, q, d):
        return across(c, q, sources[d], relay_send.at[c, q, d], relay_recv.at[c, q, d], sibling)

    every = [(c, q) for c in range(chunks) for q in range(PIECES)]
    for c, q in every:
        swap(0, c, q).start()

    copy.wait()

    @pl.loop(0, block_rows)
    def _(i):
        for k in range(0, slots, 2):
            pair = [ham[i, s] * live_ref[i, s] for s in (k, k + 1)]
            hi, lo = split(jnp.concatenate(pair, axis=1))
            mats[i, k // 2, pl.ds(0, size), :] = hi
            mats[i, k // 2, pl.ds(size, size), :] = lo

    def spread(read, place, q):
        @pl.loop(0, piece // size)
        def _(b):
            at = pl.multiple_of(q * piece + b * size, size)
            hi, lo = split(read(pl.ds(at, size)))
            to = (place * rows + q * piece) // size + b
            hi_ref[to] = hi
            lo_ref[to] = lo

    def forward(stage, c, q):
        swap(stage, c, q).wait_recv()
        pass_on(stage, c, q).start()

    def relay_all(c, q):
        for d in range(len(overs)):
            over(c, q, d).wait_recv()
            relay(c, q, d).start()

    order = [(stage, c) for stage in range(2) for c in range(chunks)]
    for q in range(PIECES):
        forward(0, 0, q)
    for turn, (stage, c) in enumerate(order):
        wide = pl.ds(c * width, width)

        def own(at):
            return first[c, at, :] if stage else vec_ref[at, wide]

        for q in range(PIECES):
            spread(own, 0, q)
            spread(lambda at: near[stage, c, at, :], 1, q)
        for q in range(PIECES):
            pass_on(stage, c, q).wait_recv()
            spread(lambda at: far[stage, c, at, :], 2, q)

        for q in range(PIECES):
            @pl.loop(q * block_rows // PIECES, (q + 1) * block_rows // PIECES)
            def _(i):
                total = jnp.zeros((size, width), jnp.float32)
                for k in range(0, slots, 2):
                    vhi = jnp.concatenate([hi_ref[pos_ref[i, s]] for s in (k, k + 1)], axis=0)
                    vlo = jnp.concatenate([lo_ref[pos_ref[i, s]] for s in (k, k + 1)], axis=0)
                    both = dot(mats[i, k // 2], vhi)
                    total += both[:size] + both[size:] + dot(mats[i, k // 2, pl.ds(0, size), :], vlo)
                at = pl.ds(pl.multiple_of(i * size, size), size)
                out = (total - coef_ref[0] * own(at)) / coef_ref[1]
                if stage:
                    full_ref[at, columns(c, vec)] = 2 * out - vec_ref[at, wide]
                else:
                    first[c, at, :] = out

            if stage:
                for d in range(len(overs)):
                    over(c, q, d).start()
                side(c, q).start()
            else:
                swap(1, c, q).start()
            if turn + 1 < len(order):
                forward(*order[turn + 1], q)
            elif chunks > 1:
                relay_all(0, q)

    for c, q in every:
        if c > 0 or chunks == 1:
            relay_all(c, q)
    for c, q in every:
        side(c, q).wait()
        for d in range(len(overs)):
            over(c, q, d).wait_send()
            relay(c, q, d).wait()
        for stage in range(2):
            swap(stage, c, q).wait_send()
            pass_on(stage, c, q).wait_send()


def filtered_rows(row_count, vec_count, width, pos, live, coef, vectors, ham):
    rows, cols = vectors.shape
    block_rows, slots, size, _ = ham.shape
    chunks = cols // width
    smem = pl.BlockSpec(memory_space=pltpu.SMEM)
    vmem = pl.BlockSpec(memory_space=pltpu.VMEM)
    dma = pltpu.SemaphoreType.DMA
    others = max(1, vec_count // 2 - 1)
    return pl.pallas_call(
        functools.partial(filter_kernel, row_count, vec_count, width),
        out_shape=jax.ShapeDtypeStruct((rows, cols * vec_count), jnp.float32),
        in_specs=[smem, smem, smem, vmem, pl.BlockSpec(memory_space=pl.ANY)],
        out_specs=vmem,
        scratch_shapes=[
            pltpu.VMEM(ham.shape, jnp.float32),
            pltpu.VMEM((block_rows, slots // 2, 2 * size, 2 * size), jnp.bfloat16),
            pltpu.VMEM((2, chunks, rows, width), jnp.float32),
            pltpu.VMEM((2, chunks, rows, width), jnp.float32),
            pltpu.VMEM((chunks, rows, width), jnp.float32),
            pltpu.VMEM((3 * block_rows, size, width), jnp.bfloat16),
            pltpu.VMEM((3 * block_rows, size, width), jnp.bfloat16),
            dma,
            dma((2, chunks, PIECES)), dma((2, chunks, PIECES)),
            dma((2, chunks, PIECES)), dma((2, chunks, PIECES)),
            dma((chunks, PIECES)), dma((chunks, PIECES)),
            dma((chunks, PIECES, others)), dma((chunks, PIECES, others)),
            dma((chunks, PIECES, others)), dma((chunks, PIECES, others)),
        ],
        compiler_params=pltpu.CompilerParams(
            collective_id=0, has_side_effects=True, vmem_limit_bytes=58 * 1024 * 1024
        ),
    )(pos, live, coef, vectors, ham)


def gram_kernel(row_count, vec_count, width, full_ref, gram_ref, hi_ref, lo_ref, own_ref, panel, inbox,
                sum_send, sum_recv, deep_send, deep_recv, swap_send, swap_recv, over_send, over_recv,
                side_send, side_recv):
    row, vec = lax.axis_index("row"), lax.axis_index("vec")
    rows, all_cols = full_ref.shape
    chunks, span = all_cols // vec_count // width, width * vec_count
    piece = panel.shape[0] // row_count
    pairs, groups = row_count // 2, vec_count // 2
    partner = row + 1 - 2 * (row % 2)
    sibling = vec + 1 - 2 * (vec % 2)

    barrier = pltpu.get_barrier_semaphore()
    peers = [((row + d) % row_count, vec) for d in range(1, row_count)]
    peers += [(row, (vec + 2 * d) % vec_count) for d in range(1, groups)] + [(row, sibling)]
    for peer in peers:
        pl.semaphore_signal(barrier, inc=1, device_id=peer, device_id_type=MESH)

    step = 128

    @pl.loop(0, rows // step)
    def _(b):
        at = pl.ds(pl.multiple_of(b * step, step), step)
        hi, lo = split(full_ref[at, :])
        hi_ref[at, :] = hi
        lo_ref[at, :] = lo
        for c in range(chunks):
            mine = full_ref[at, pl.ds(pl.multiple_of(c * span + vec * width, width), width)].T
            hi, lo = split(mine)
            own_ref[c, pl.ds(0, width), at] = hi
            own_ref[c, pl.ds(width, width), at] = lo

    def give(d):
        target = (row + d) % row_count
        return pltpu.make_async_remote_copy(
            panel.at[pl.ds(pl.multiple_of(target * piece, piece), piece)], inbox.at[d - 1],
            sum_send.at[d - 1], sum_recv.at[d - 1], device_id=(target, vec), device_id_type=MESH)

    tile = min(256, all_cols)
    for c in range(chunks):
        @pl.loop(0, all_cols // tile)
        def _(t):
            at = pl.ds(pl.multiple_of(t * tile, tile), tile)
            both = dot(own_ref[c], hi_ref[:, at])
            panel[pl.ds(c * width, width), at] = (
                both[:width] + both[width:] + dot(own_ref[c, pl.ds(0, width), :], lo_ref[:, at])
            )
    pl.semaphore_wait(barrier, len(peers))
    for d in range(1, row_count):
        give(d).start()

    def rows_of(r, v):
        local = r * piece
        return pl.ds(pl.multiple_of(local // width * span + v * width + local % width, piece), piece)

    def send(r, v, sems, index, to):
        at = gram_ref.at[rows_of(r, v)]
        return pltpu.make_async_remote_copy(
            at, at, sems[0].at[index], sems[1].at[index], device_id=to, device_id_type=MESH)

    def row_of(k, base):
        return (base + 2 * k) % row_count

    def deep(d):
        return send(row, vec, (deep_send, deep_recv), d - 1, (row_of(d, row), vec))

    def swap(k):
        return send(row_of(k, row), vec, (swap_send, swap_recv), k, (partner, vec))

    def held(k):
        return row_of(k, row) if k < pairs else row_of(k - pairs, partner)

    def over(k, d):
        return send(held(k), vec, (over_send, over_recv), (k, d - 1), (row, (vec + 2 * d) % vec_count))

    def side(k, d):
        return send(held(k), (vec + 2 * d) % vec_count, (side_send, side_recv), (k, d), (row, sibling))

    acc = panel[pl.ds(pl.multiple_of(row * piece, piece), piece), :]
    for d in range(1, row_count):
        give(d).wait_recv()
        acc = acc + inbox[d - 1]
    gram_ref[rows_of(row, vec), :] = acc
    for d in range(1, pairs):
        deep(d).start()

    def spread(k):
        for d in range(1, groups):
            over(k, d).start()
        side(k, 0).start()

    swap(0).start()
    spread(0)
    for d in range(1, pairs):
        deep(pairs - d).wait_recv()
        swap(d).start()
        spread(d)
    for k in range(pairs):
        swap(k).wait_recv()
        spread(pairs + k)
    for k in range(row_count):
        for d in range(1, groups):
            over(k, groups - d).wait_recv()
            side(k, d).start()
    for d in range(1, row_count):
        give(d).wait_send()
    for d in range(1, pairs):
        deep(d).wait_send()
    for k in range(pairs):
        swap(k).wait_send()
    for k in range(row_count):
        for d in range(1, groups):
            over(k, d).wait_send()
        for d in range(groups):
            side(k, d).wait()


def full_gram(row_count, vec_count, width, full):
    rows, all_cols = full.shape
    cols = all_cols // vec_count
    vmem = pl.BlockSpec(memory_space=pltpu.VMEM)
    dma = pltpu.SemaphoreType.DMA
    pairs, groups = row_count // 2, vec_count // 2
    others = max(1, groups - 1)
    return pl.pallas_call(
        functools.partial(gram_kernel, row_count, vec_count, width),
        out_shape=jax.ShapeDtypeStruct((all_cols, all_cols), jnp.float32),
        in_specs=[vmem],
        out_specs=vmem,
        scratch_shapes=[
            pltpu.VMEM((rows, all_cols), jnp.bfloat16),
            pltpu.VMEM((rows, all_cols), jnp.bfloat16),
            pltpu.VMEM((cols // width, 2 * width, rows), jnp.bfloat16),
            pltpu.VMEM((cols, all_cols), jnp.float32),
            pltpu.VMEM((row_count - 1, cols // row_count, all_cols), jnp.float32),
            dma((row_count - 1,)), dma((row_count - 1,)),
            dma((max(1, pairs - 1),)), dma((max(1, pairs - 1),)),
            dma((pairs,)), dma((pairs,)),
            dma((row_count, others)), dma((row_count, others)),
            dma((row_count, groups)), dma((row_count, groups)),
        ],
        compiler_params=pltpu.CompilerParams(
            collective_id=1, has_side_effects=True, vmem_limit_bytes=50 * 1024 * 1024
        ),
    )(full)


def on_device(vectors, hamiltonian, column_blocks, live_counts, lower_bound, upper_bound):
    rows_dev, panel_cols = vectors.shape
    block_rows = hamiltonian.shape[0]
    row_count = lax.axis_size("row")
    vec_count = lax.axis_size("vec")
    me = lax.axis_index("row")
    all_cols = panel_cols * vec_count

    rel = (column_blocks - me * block_rows + block_rows) % (block_rows * row_count)
    side = rel // block_rows
    part = jnp.where(side == 1, 0, jnp.where((side == 2) == (me % 2 == 0), 1, 2))
    pos = part * block_rows + rel % block_rows
    slots = column_blocks.shape[1]
    live = (jnp.arange(slots, dtype=jnp.int32)[None, :] < live_counts[:, None]).astype(jnp.float32)
    centre = (upper_bound[0] + lower_bound[0]) / 2
    radius = (upper_bound[0] - lower_bound[0]) / 2
    coef = jnp.stack([centre, radius])

    width = max(128, panel_cols // 2)
    full_rows = filtered_rows(
        row_count, vec_count, width, pos, live, coef, vectors, hamiltonian
    )

    high = lax.Precision.HIGH
    span = width * vec_count
    gram = full_gram(row_count, vec_count, width, full_rows)
    panel = jnp.concatenate([
        lax.dynamic_slice_in_dim(gram, c * span + lax.axis_index("vec") * width, width, axis=1)
        for c in range(panel_cols // width)
    ], axis=1)
    energy = jnp.trace(gram)
    scale2 = all_cols / (4 * (energy + 1e-06))
    gram = gram * scale2
    local = jnp.arange(panel_cols)
    column = local // width * (width * vec_count) + lax.axis_index("vec") * width + local % width
    eye = (jnp.arange(all_cols)[:, None] == column[None, :]).astype(jnp.float32)

    def times_gram(level, x):
        if level == 0:
            return jnp.dot(gram, x, precision=high)
        return times_gram(level - 1, times_step(level - 1, times_step(level - 1, x)))

    def times_step(level, x):
        return 1.5 * x - 0.5 * times_gram(level, x)

    poly = 1.5 * eye - 0.5 * panel * scale2
    for level in range(1, NS_ITERS):
        poly = times_step(level, poly)
    poly = poly * (jnp.sqrt(scale2) * math.sqrt(rows_dev * row_count))
    return jnp.dot(full_rows, poly, precision=high)


def solution(mesh):
    placed = (P("row", "vec"), P("row", None, None, None), P("row", None), P("row"), P(), P())
    return jax.shard_map(
        on_device, mesh=mesh, in_specs=placed, out_specs=P("row", "vec"), check_vma=False
    )
```

```python
import functools
import math

import jax
import jax.numpy as jnp
from jax import lax
from jax.experimental import pallas as pl
from jax.experimental.pallas import tpu as pltpu
from jax.sharding import PartitionSpec as P

NS_ITERS = 3
PIECES = 4
MESH = pl.DeviceIdType.MESH


def split(x):
    hi = x.astype(jnp.bfloat16)
    return hi, (x - hi.astype(jnp.float32)).astype(jnp.bfloat16)


def dot(a, b):
    return jnp.dot(a, b, preferred_element_type=jnp.float32)


def filter_kernel(row_count, vec_count, width, pos_ref, live_ref, coef_ref, vec_ref, ham_ref, full_ref,
                  ham, mats, near, far, first, hi_ref, lo_ref, ham_sem,
                  swap_send, swap_recv, pass_send, pass_recv, side_send, side_recv, over_send, over_recv,
                  relay_send, relay_recv):
    row, vec = lax.axis_index("row"), lax.axis_index("vec")
    rows, cols = vec_ref.shape
    block_rows, slots, size, _ = ham.shape
    chunks = cols // width
    piece = rows // PIECES
    even = 1 - row % 2
    partner = row + 2 * even - 1
    onward = (row + 4 * even - 2 + row_count) % row_count
    backward = (row - 4 * even + 2 + row_count) % row_count
    sibling = vec + 1 - 2 * (vec % 2)
    overs = [(vec + 2 * d) % vec_count for d in range(1, vec_count // 2)]
    sources = [(vec - 2 * d + vec_count) % vec_count for d in range(1, vec_count // 2)]

    copy = pltpu.make_async_copy(ham_ref, ham, ham_sem)
    copy.start()
    barrier = pltpu.get_barrier_semaphore()
    peers = [(partner, vec), (onward, vec), (backward, vec), (row, sibling)] + [(row, v) for v in overs]
    for peer in peers:
        pl.semaphore_signal(barrier, inc=1, device_id=peer, device_id_type=MESH)
    pl.semaphore_wait(barrier, len(peers))

    def part(q):
        return pl.ds(q * piece, piece)

    def columns(c, v):
        return pl.ds(pl.multiple_of((c * vec_count + v) * width, width), width)

    def own_at(stage, c, q):
        return first.at[c, part(q)] if stage else vec_ref.at[part(q), pl.ds(c * width, width)]

    def swap(stage, c, q):
        return pltpu.make_async_remote_copy(
            own_at(stage, c, q), near.at[stage, c, part(q)], swap_send.at[stage, c, q], swap_recv.at[stage, c, q],
            device_id=(partner, vec), device_id_type=MESH)

    def pass_on(stage, c, q):
        return pltpu.make_async_remote_copy(
            near.at[stage, c, part(q)], far.at[stage, c, part(q)], pass_send.at[stage, c, q],
            pass_recv.at[stage, c, q], device_id=(onward, vec), device_id_type=MESH)

    def across(c, q, v, send, recv, to):
        at = full_ref.at[part(q), columns(c, v)]
        return pltpu.make_async_remote_copy(at, at, send, recv, device_id=(row, to), device_id_type=MESH)

    def side(c, q):
        return across(c, q, vec, side_send.at[c, q], side_recv.at[c, q], sibling)

    def over(c, q, d):
        return across(c, q, vec, over_send.at[c, q, d], over_recv.at[c, q, d], overs[d])

    def relay(c, q, d):
        return across(c, q, sources[d], relay_send.at[c, q, d], relay_recv.at[c, q, d], sibling)

    every = [(c, q) for c in range(chunks) for q in range(PIECES)]
    for c, q in every[:3]:
        swap(0, c, q).start()

    copy.wait()

    @pl.loop(0, block_rows)
    def _(i):
        for k in range(0, slots, 2):
            pair = [ham[i, s] * live_ref[i, s] for s in (k, k + 1)]
            hi, lo = split(jnp.concatenate(pair, axis=1))
            mats[i, k // 2, pl.ds(0, size), :] = hi
            mats[i, k // 2, pl.ds(size, size), :] = lo

    def spread(read, place, q):
        @pl.loop(0, piece // size)
        def _(b):
            at = pl.multiple_of(q * piece + b * size, size)
            hi, lo = split(read(pl.ds(at, size)))
            to = (place * rows + q * piece) // size + b
            hi_ref[to] = hi
            lo_ref[to] = lo

    def forward(stage, c, q):
        swap(stage, c, q).wait_recv()
        pass_on(stage, c, q).start()
        later = c * PIECES + q + 3
        if stage == 0 and later < len(every):
            swap(0, *every[later]).start()

    def relay_all(c, q):
        for d in range(len(overs)):
            over(c, q, d).wait_recv()
            relay(c, q, d).start()

    order = [(stage, c) for stage in range(2) for c in range(chunks)]
    for q in range(PIECES):
        forward(0, 0, q)
    for turn, (stage, c) in enumerate(order):
        wide = pl.ds(c * width, width)

        def own(at):
            return first[c, at, :] if stage else vec_ref[at, wide]

        for q in range(PIECES):
            spread(own, 0, q)
            spread(lambda at: near[stage, c, at, :], 1, q)
        for q in range(PIECES):
            pass_on(stage, c, q).wait_recv()
            spread(lambda at: far[stage, c, at, :], 2, q)

        for q in range(PIECES):
            @pl.loop(q * block_rows // PIECES, (q + 1) * block_rows // PIECES)
            def _(i):
                total = jnp.zeros((size, width), jnp.float32)
                for k in range(0, slots, 2):
                    vhi = jnp.concatenate([hi_ref[pos_ref[i, s]] for s in (k, k + 1)], axis=0)
                    vlo = jnp.concatenate([lo_ref[pos_ref[i, s]] for s in (k, k + 1)], axis=0)
                    both = dot(mats[i, k // 2], vhi)
                    total += both[:size] + both[size:] + dot(mats[i, k // 2, pl.ds(0, size), :], vlo)
                at = pl.ds(pl.multiple_of(i * size, size), size)
                out = (total - coef_ref[0] * own(at)) / coef_ref[1]
                if stage:
                    full_ref[at, columns(c, vec)] = 2 * out - vec_ref[at, wide]
                else:
                    first[c, at, :] = out

            if stage:
                for d in range(len(overs)):
                    over(c, q, d).start()
                side(c, q).start()
            else:
                swap(1, c, q).start()
            if turn + 1 < len(order):
                forward(*order[turn + 1], q)
            elif chunks > 1:
                relay_all(0, q)

    for c, q in every:
        if c > 0 or chunks == 1:
            relay_all(c, q)
    for c, q in every:
        side(c, q).wait()
        for d in range(len(overs)):
            over(c, q, d).wait_send()
            relay(c, q, d).wait()
        for stage in range(2):
            swap(stage, c, q).wait_send()
            pass_on(stage, c, q).wait_send()


def filtered_rows(row_count, vec_count, width, pos, live, coef, vectors, ham):
    rows, cols = vectors.shape
    block_rows, slots, size, _ = ham.shape
    chunks = cols // width
    smem = pl.BlockSpec(memory_space=pltpu.SMEM)
    vmem = pl.BlockSpec(memory_space=pltpu.VMEM)
    dma = pltpu.SemaphoreType.DMA
    others = max(1, vec_count // 2 - 1)
    return pl.pallas_call(
        functools.partial(filter_kernel, row_count, vec_count, width),
        out_shape=jax.ShapeDtypeStruct((rows, cols * vec_count), jnp.float32),
        in_specs=[smem, smem, smem, vmem, pl.BlockSpec(memory_space=pl.ANY)],
        out_specs=vmem,
        scratch_shapes=[
            pltpu.VMEM(ham.shape, jnp.float32),
            pltpu.VMEM((block_rows, slots // 2, 2 * size, 2 * size), jnp.bfloat16),
            pltpu.VMEM((2, chunks, rows, width), jnp.float32),
            pltpu.VMEM((2, chunks, rows, width), jnp.float32),
            pltpu.VMEM((chunks, rows, width), jnp.float32),
            pltpu.VMEM((3 * block_rows, size, width), jnp.bfloat16),
            pltpu.VMEM((3 * block_rows, size, width), jnp.bfloat16),
            dma,
            dma((2, chunks, PIECES)), dma((2, chunks, PIECES)),
            dma((2, chunks, PIECES)), dma((2, chunks, PIECES)),
            dma((chunks, PIECES)), dma((chunks, PIECES)),
            dma((chunks, PIECES, others)), dma((chunks, PIECES, others)),
            dma((chunks, PIECES, others)), dma((chunks, PIECES, others)),
        ],
        compiler_params=pltpu.CompilerParams(
            collective_id=0, has_side_effects=True, vmem_limit_bytes=58 * 1024 * 1024
        ),
    )(pos, live, coef, vectors, ham)


def gram_kernel(row_count, vec_count, width, full_ref, gram_ref, hi_ref, lo_ref, own_ref, panel, inbox,
                sum_send, sum_recv, deep_send, deep_recv, swap_send, swap_recv, over_send, over_recv,
                side_send, side_recv):
    row, vec = lax.axis_index("row"), lax.axis_index("vec")
    rows, all_cols = full_ref.shape
    chunks, span = all_cols // vec_count // width, width * vec_count
    piece = panel.shape[0] // row_count
    pairs, groups = row_count // 2, vec_count // 2
    partner = row + 1 - 2 * (row % 2)
    sibling = vec + 1 - 2 * (vec % 2)

    barrier = pltpu.get_barrier_semaphore()
    peers = [((row + d) % row_count, vec) for d in range(1, row_count)]
    peers += [(row, (vec + 2 * d) % vec_count) for d in range(1, groups)] + [(row, sibling)]
    for peer in peers:
        pl.semaphore_signal(barrier, inc=1, device_id=peer, device_id_type=MESH)

    step = 128

    @pl.loop(0, rows // step)
    def _(b):
        at = pl.ds(pl.multiple_of(b * step, step), step)
        hi, lo = split(full_ref[at, :])
        hi_ref[at, :] = hi
        lo_ref[at, :] = lo
        for c in range(chunks):
            mine = full_ref[at, pl.ds(pl.multiple_of(c * span + vec * width, width), width)].T
            hi, lo = split(mine)
            own_ref[c, pl.ds(0, width), at] = hi
            own_ref[c, pl.ds(width, width), at] = lo

    def give(d):
        target = (row + d) % row_count
        return pltpu.make_async_remote_copy(
            panel.at[pl.ds(pl.multiple_of(target * piece, piece), piece)], inbox.at[d - 1],
            sum_send.at[d - 1], sum_recv.at[d - 1], device_id=(target, vec), device_id_type=MESH)

    tile = min(256, all_cols)
    for c in range(chunks):
        @pl.loop(0, all_cols // tile)
        def _(t):
            at = pl.ds(pl.multiple_of(t * tile, tile), tile)
            both = dot(own_ref[c], hi_ref[:, at])
            panel[pl.ds(c * width, width), at] = (
                both[:width] + both[width:] + dot(own_ref[c, pl.ds(0, width), :], lo_ref[:, at])
            )
    pl.semaphore_wait(barrier, len(peers))
    for d in range(1, row_count):
        give(d).start()

    def rows_of(r, v):
        local = r * piece
        return pl.ds(pl.multiple_of(local // width * span + v * width + local % width, piece), piece)

    def send(r, v, sems, index, to):
        at = gram_ref.at[rows_of(r, v)]
        return pltpu.make_async_remote_copy(
            at, at, sems[0].at[index], sems[1].at[index], device_id=to, device_id_type=MESH)

    def row_of(k, base):
        return (base + 2 * k) % row_count

    def deep(d):
        return send(row, vec, (deep_send, deep_recv), d - 1, (row_of(d, row), vec))

    def swap(k):
        return send(row_of(k, row), vec, (swap_send, swap_recv), k, (partner, vec))

    def held(k):
        return row_of(k, row) if k < pairs else row_of(k - pairs, partner)

    def over(k, d):
        return send(held(k), vec, (over_send, over_recv), (k, d - 1), (row, (vec + 2 * d) % vec_count))

    def side(k, d):
        return send(held(k), (vec + 2 * d) % vec_count, (side_send, side_recv), (k, d), (row, sibling))

    acc = panel[pl.ds(pl.multiple_of(row * piece, piece), piece), :]
    for d in range(1, row_count):
        give(d).wait_recv()
        acc = acc + inbox[d - 1]
    gram_ref[rows_of(row, vec), :] = acc
    for d in range(1, pairs):
        deep(d).start()

    def spread(k):
        for d in range(1, groups):
            over(k, d).start()
        side(k, 0).start()

    swap(0).start()
    spread(0)
    for d in range(1, pairs):
        deep(pairs - d).wait_recv()
        swap(d).start()
        spread(d)
    for k in range(pairs):
        swap(k).wait_recv()
        spread(pairs + k)
    for k in range(row_count):
        for d in range(1, groups):
            over(k, groups - d).wait_recv()
            side(k, d).start()
    for d in range(1, row_count):
        give(d).wait_send()
    for d in range(1, pairs):
        deep(d).wait_send()
    for k in range(pairs):
        swap(k).wait_send()
    for k in range(row_count):
        for d in range(1, groups):
            over(k, d).wait_send()
        for d in range(groups):
            side(k, d).wait()


def full_gram(row_count, vec_count, width, full):
    rows, all_cols = full.shape
    cols = all_cols // vec_count
    vmem = pl.BlockSpec(memory_space=pltpu.VMEM)
    dma = pltpu.SemaphoreType.DMA
    pairs, groups = row_count // 2, vec_count // 2
    others = max(1, groups - 1)
    return pl.pallas_call(
        functools.partial(gram_kernel, row_count, vec_count, width),
        out_shape=jax.ShapeDtypeStruct((all_cols, all_cols), jnp.float32),
        in_specs=[vmem],
        out_specs=vmem,
        scratch_shapes=[
            pltpu.VMEM((rows, all_cols), jnp.bfloat16),
            pltpu.VMEM((rows, all_cols), jnp.bfloat16),
            pltpu.VMEM((cols // width, 2 * width, rows), jnp.bfloat16),
            pltpu.VMEM((cols, all_cols), jnp.float32),
            pltpu.VMEM((row_count - 1, cols // row_count, all_cols), jnp.float32),
            dma((row_count - 1,)), dma((row_count - 1,)),
            dma((max(1, pairs - 1),)), dma((max(1, pairs - 1),)),
            dma((pairs,)), dma((pairs,)),
            dma((row_count, others)), dma((row_count, others)),
            dma((row_count, groups)), dma((row_count, groups)),
        ],
        compiler_params=pltpu.CompilerParams(
            collective_id=1, has_side_effects=True, vmem_limit_bytes=50 * 1024 * 1024
        ),
    )(full)


def finish_kernel(total_rows, span, width, vec_ref, full_ref, gram_ref, out_ref, ghi, glo, xhi, xlo, *bufs):
    vec = vec_ref[0]
    rows, all_cols = full_ref.shape
    cols = out_ref.shape[1]
    step = 128
    diagonal = (
        lax.broadcasted_iota(jnp.int32, (step, step), 0) == lax.broadcasted_iota(jnp.int32, (step, step), 1)
    ).astype(jnp.float32)
    energy = jnp.zeros((step, step), jnp.float32)
    for b in range(0, all_cols, step):
        energy += gram_ref[pl.ds(b, step), pl.ds(b, step)] * diagonal
    energy = jnp.sum(jnp.sum(energy, axis=1, keepdims=True), axis=0, keepdims=True)
    scale2 = all_cols / (4 * (energy + 1e-06))
    poly, spare = bufs[:2]

    @pl.loop(0, all_cols // step)
    def _(b):
        at = pl.ds(pl.multiple_of(b * step, step), step)
        ghi[at, :], glo[at, :] = split(gram_ref[at, :] * scale2)
        for c in range(cols // width):
            first_col = pl.multiple_of(c * span + vec * width, width)
            row_ids = b * step + lax.broadcasted_iota(jnp.int32, (step, width), 0)
            col_ids = first_col + lax.broadcasted_iota(jnp.int32, (step, width), 1)
            eye = (row_ids == col_ids).astype(jnp.float32)
            poly[at, pl.ds(c * width, width)] = 1.5 * eye - 0.5 * (gram_ref[at, pl.ds(first_col, width)] * scale2)

    tile = 256

    def three(hi, lo):
        return dot(hi, xhi[...]) + dot(lo, xhi[...]) + dot(hi, xlo[...])

    def times_gram(level, dst, src, base):
        if level == 0:
            xhi[...], xlo[...] = split(src[...])

            @pl.loop(0, all_cols // tile)
            def _(t):
                at = pl.ds(pl.multiple_of(t * tile, tile), tile)
                out = three(ghi[at, :], glo[at, :])
                dst[at, :] = out if base is None else 1.5 * base[at, :] - 0.5 * out
            return
        one, two = bufs[2 * level], bufs[2 * level + 1]
        times_step(level - 1, one, src)
        times_step(level - 1, two, one)
        times_gram(level - 1, dst, two, base)

    def times_step(level, dst, src):
        times_gram(level, dst, src, src)

    for level in range(1, NS_ITERS):
        times_step(level, spare, poly)
        poly, spare = spare, poly
    xhi[...], xlo[...] = split(poly[...] * (jnp.sqrt(scale2) * math.sqrt(total_rows)))

    @pl.loop(0, rows // tile)
    def _(t):
        at = pl.ds(pl.multiple_of(t * tile, tile), tile)
        out_ref[at, :] = three(*split(full_ref[at, :]))


def finish(total_rows, span, width, vec, cols, full, gram):
    rows, all_cols = full.shape
    vmem = pl.BlockSpec(memory_space=pltpu.VMEM)
    return pl.pallas_call(
        functools.partial(finish_kernel, total_rows, span, width),
        out_shape=jax.ShapeDtypeStruct((rows, cols), jnp.float32),
        in_specs=[pl.BlockSpec(memory_space=pltpu.SMEM), vmem, vmem],
        out_specs=vmem,
        scratch_shapes=[pltpu.VMEM((all_cols, all_cols), jnp.bfloat16)] * 2
        + [pltpu.VMEM((all_cols, cols), jnp.bfloat16)] * 2
        + [pltpu.VMEM((all_cols, cols), jnp.float32)] * (2 * NS_ITERS),
        compiler_params=pltpu.CompilerParams(vmem_limit_bytes=50 * 1024 * 1024),
    )(vec, full, gram)


def on_device(vectors, hamiltonian, column_blocks, live_counts, lower_bound, upper_bound):
    rows_dev, panel_cols = vectors.shape
    block_rows = hamiltonian.shape[0]
    row_count = lax.axis_size("row")
    vec_count = lax.axis_size("vec")
    me = lax.axis_index("row")

    rel = (column_blocks - me * block_rows + block_rows) % (block_rows * row_count)
    side = rel // block_rows
    part = jnp.where(side == 1, 0, jnp.where((side == 2) == (me % 2 == 0), 1, 2))
    pos = part * block_rows + rel % block_rows
    slots = column_blocks.shape[1]
    live = (jnp.arange(slots, dtype=jnp.int32)[None, :] < live_counts[:, None]).astype(jnp.float32)
    centre = (upper_bound[0] + lower_bound[0]) / 2
    radius = (upper_bound[0] - lower_bound[0]) / 2
    coef = jnp.stack([centre, radius])

    width = max(128, panel_cols // 2)
    full_rows = filtered_rows(
        row_count, vec_count, width, pos, live, coef, vectors, hamiltonian
    )

    span = width * vec_count
    gram = full_gram(row_count, vec_count, width, full_rows)
    vec = jnp.full((1,), lax.axis_index("vec"), jnp.int32)
    return finish(rows_dev * row_count, span, width, vec, panel_cols, full_rows, gram)


def solution(mesh):
    placed = (P("row", "vec"), P("row", None, None, None), P("row", None), P("row"), P(), P())
    return jax.shard_map(
        on_device, mesh=mesh, in_specs=placed, out_specs=P("row", "vec"), check_vma=False
    )
```
